256 devices in a mesh: dp: 8 (over x, y_lo), seq: 32 (over z, y_hi, core).
Axes of the slice: x: 4, y: 4 (y_hi: 2, y_lo: 2; y = y_hi * 2 + y_lo), z: 8, core: 2. Of those that a mesh axis runs over, the one named last changes fastest.
Arguments:
- tokens: float32 [8, 16384, 512], P('dp', 'seq'), may hold values from -6 to 6
- in_weight: float32 [512, 1024], P('dp'), may hold values from -0.25 to 0.25
- filters: float32 [16384, 512], P('seq'), may hold values from -1.5 to 1.5
- cotangent: float32 [8, 16384, 512], P('dp', 'seq'), may hold values from -6 to 6
Outputs:
- mixed: float32 [8, 16384, 512], P('dp', 'seq')
- token_grad: float32 [8, 16384, 512], P('dp', 'seq')
- weight_grad: float32 [512, 1024], P('dp')
The draws below stay inside these ranges and needn't reach their ends.
All inputs are finite; a program needn't handle non-finite values.
Results may differ from the reference program's by a relative error of at most 0.00011.
Values sent between devices are 32-bit elements; how exact they have to be, the bound alone decides.
A program may use at most 128 MiB of HBM per device.

```python
import math
import jax
import jax.numpy as jnp
from jax import lax

D = 512
BATCH = 8
SEQ_LEN = 16384
TOKENS = 131072


def draw_filters(key, part):
    noise_key = jax.random.fold_in(key, 11)
    rate_key = jax.random.fold_in(key, 12)
    rates = jnp.exp(jax.random.uniform(rate_key, (D,), jnp.float32, math.log(0.1 / SEQ_LEN), math.log(1.0 / 30.0)))
    noise = jnp.clip(jax.random.normal(noise_key, (SEQ_LEN, D), jnp.float32), -4.0, 4.0)
    lags = jnp.arange(SEQ_LEN, dtype=jnp.float32)
    envelope = jnp.exp(-rates[None, :] * lags[:, None])
    scale_vals = jnp.sqrt(jnp.expm1(-2.0 * rates) / jnp.expm1(-2.0 * rates * SEQ_LEN))
    return (noise * envelope * scale_vals[None, :]).astype(jnp.float32)


def raised(values, key, source, target, shards_of, factor):
    def block_of(dim):
        return (jnp.arange(values.shape[dim]) // (values.shape[dim] // shards_of)).reshape((-1,) + (1,) * (values.ndim - 1 - dim))

    one_side = jax.random.permutation(key, shards_of)[block_of(target)]
    other_side = (block_of(target) + shards_of // 2) % shards_of
    return jnp.where((block_of(source) == one_side) | (block_of(source) == other_side), factor * values, values)


def level_of(key, dims, cuts, low, largest):
    gain = 1.0
    for position, parts in cuts:
        draws = jax.random.uniform(jax.random.fold_in(jax.random.fold_in(key, 6), position), (parts,), jnp.float32, low / len(cuts), largest / len(cuts))
        gain = gain * jnp.repeat(jnp.exp(draws), dims[position] // parts).reshape((-1,) + (1,) * (len(dims) - 1 - position))
    return gain


def centred(rng, shape, deviation, most, shards=(), kind=jnp.bfloat16):
    drawn = deviation * jax.random.normal(rng, shape, jnp.float32)
    if shards:
        drawn = drawn * level_of(rng, shape, shards, -0.22, 0.18)
    return jnp.clip(drawn, -most, most).astype(kind)


def bell_draw_with(key, extent, spread, most, shards, heavy, kind=jnp.bfloat16):
    entries = spread * jax.random.normal(key, extent, jnp.float32)
    if shards:
        entries = entries * level_of(key, extent, shards, -0.22, 0.18)
    return jnp.clip(raised(entries, jax.random.fold_in(key, 3), *heavy), -most, most).astype(kind)


def setup_inputs(seed: int = 0) -> dict:
    key_list = jax.random.split(jax.random.key(seed), 5)
    return {
        "tokens": bell_draw_with(key_list[0], (BATCH, SEQ_LEN, D), 1.0, 6.0, ((0, 8), (1, 32)), (1, 2, 32, 2.75), jnp.float32),
        "in_weight": centred(key_list[1], (D, 2 * D), D ** -0.5, 0.25, ((0, 8),), jnp.float32),
        "filters": draw_filters(jax.random.fold_in(key_list[4], 71), 0),
        "cotangent": centred(key_list[3], (BATCH, SEQ_LEN, D), 1.0, 6.0, ((0, 8), (1, 32)), jnp.float32),
    }


precise = lax.Precision.HIGHEST

def reference(tokens, in_weight, filters, cotangent):
    channels = tokens.shape[2]
    length = tokens.shape[1]
    projected = jnp.einsum('bld,de->ble', tokens, in_weight, precision=precise)
    value_part = projected[..., :channels]
    gate_part = projected[..., channels:]
    filter_spec = jnp.fft.rfft(filters, axis=0)[None]
    convolved = jnp.fft.irfft(jnp.fft.rfft(value_part, axis=1) * filter_spec, n=length, axis=1).astype(tokens.dtype)
    mixed = gate_part * convolved
    d_conv = cotangent * gate_part
    d_gate = cotangent * convolved
    d_value = jnp.fft.irfft(jnp.fft.rfft(d_conv, axis=1) * jnp.conj(filter_spec), n=length, axis=1).astype(tokens.dtype)
    d_pre = jnp.concatenate([d_value, d_gate], axis=2)
    token_grad = jnp.einsum('ble,de->bld', d_pre, in_weight, precision=precise)
    weight_grad = jnp.einsum('bld,ble->de', tokens, d_pre, precision=precise) / jnp.sqrt(jnp.float32(TOKENS)).astype(tokens.dtype)
    return (mixed, token_grad, weight_grad)
```

```python
import math

import jax
import jax.numpy as jnp
import numpy as np
from jax import lax
from jax.experimental import pallas as pl
from jax.experimental.pallas import tpu as pltpu
from jax.sharding import PartitionSpec as P

F32 = jnp.float32
BF16 = jnp.bfloat16
MESH = pl.DeviceIdType.MESH
CORES = 2
QUARTER = 4
CHUNK_CHANNELS = 4


def split_np(values):
    high = values.astype(np.float32).astype(jnp.bfloat16)
    low = (values - high.astype(np.float64)).astype(np.float32).astype(jnp.bfloat16)
    return high, low


def trig(rows, columns, period):
    product = np.outer(np.arange(rows), np.arange(columns)) % period
    angle = 2.0 * np.pi * product / period
    return np.cos(angle), np.sin(angle)


def tables(seq, lanes):
    n1 = QUARTER * seq
    total = n1 * lanes
    c1, s1 = trig(n1, n1, n1)
    c2, s2 = trig(lanes, lanes, lanes)
    ct, st = trig(n1, lanes, total)
    n1_of = np.arange(n1).reshape(seq, QUARTER)
    zeros = np.zeros((n1, seq, QUARTER))
    top_v = np.concatenate([c1[:, n1_of], zeros], axis=2).reshape(n1, 2 * n1)
    bot_v = np.concatenate([-s1[:, n1_of], zeros], axis=2).reshape(n1, 2 * n1)
    top_d = np.concatenate([zeros, c1[:, n1_of]], axis=2).reshape(n1, 2 * n1)
    bot_d = np.concatenate([zeros, s1[:, n1_of]], axis=2).reshape(n1, 2 * n1)
    forward1 = np.concatenate([top_v, bot_v, top_d, bot_d], axis=0)
    forward_re = np.concatenate([c2, s2], axis=0)
    forward_im = np.concatenate([c2, -s2], axis=0)
    filter2 = np.block([[c2, -s2], [s2, c2]])
    inverse2 = np.block([[c2, s2, c2, -s2], [-s2, c2, s2, c2]])
    zero = np.zeros((n1, n1))
    conv_rows = np.concatenate([c1, -s1, zero, zero], axis=1) / total
    value_rows = np.concatenate([zero, zero, -s1, c1], axis=1) / total
    inverse1 = np.stack(
        [conv_rows.reshape(seq, QUARTER, 4 * n1), value_rows.reshape(seq, QUARTER, 4 * n1)],
        axis=1,
    ).reshape(2 * n1, 4 * n1)
    halves = [
        part
        for matrix in (forward1, forward_re, forward_im, filter2, inverse2, inverse1)
        for part in split_np(matrix)
    ]
    return halves + [ct.astype(np.float32), st.astype(np.float32)]


def split(values):
    high = values.astype(BF16)
    return high, (values - high.astype(F32)).astype(BF16)


def dot3(a, b, dims=((1,), (0,))):
    def one(x, y):
        return lax.dot_general(x, y, (dims, ((), ())), preferred_element_type=F32)

    return one(a[0], b[0]) + one(a[0], b[1]) + one(a[1], b[0])


def build_kernel(dp, seq, channels, lanes, token_total):
    cc = CHUNK_CHANNELS
    width = cc * seq
    chunks = channels // width
    rows = QUARTER * lanes
    n1 = QUARTER * seq
    dp_rows = channels // dp
    half_rows = dp_rows // CORES
    chips = seq // CORES
    groups = chips // chunks
    piece = half_rows // groups
    pair_count = (chunks // 2) * cc
    assert pair_count == dp and groups * chunks == chips and piece * groups == half_rows
    scale = 1.0 / math.sqrt(token_total)

    def kernel(
        tok, w_in, filt, cot,
        f1h, f1l, frh, frl, fih, fil, g2h, g2l, i2h, i2l, i1h, i1l, ct, st,
        mixed, token_grad, weight_grad,
        wsend, wall, wh, wl, th, tl, tth, ttl, gate,
        fsend, frecv, bsend, brecv,
        ftmp, ffs, fall, spec,
        wg, sib, rsend, rrecv, rsum, precv, agsend, agrecv,
        w_s, w_r, ff_s, ff_r, fg_s, fg_r, fs, fr, bs, br,
        sib_s, sib_r, rs_s, rs_r, p_s, p_r, ag_s, ag_r,
    ):
        me_dp = lax.axis_index("dp")
        me = lax.axis_index("seq")
        core = lax.rem(me, CORES)
        chip = me // CORES
        sibling = chip * CORES + (CORES - 1 - core)

        def remote(src, dst, send, recv, d, s):
            return pltpu.make_async_remote_copy(
                src_ref=src, dst_ref=dst, send_sem=send, recv_sem=recv,
                device_id=(d, s), device_id_type=MESH,
            )

        def wait_bytes(ref, sem):
            pltpu.make_async_copy(ref, ref, sem).wait()

        barrier = pltpu.get_barrier_semaphore()

        @pl.loop(1, seq)
        def _(i):
            pl.semaphore_signal(
                barrier, inc=1, device_id=(me_dp, lax.rem(me + i, seq)), device_id_type=MESH
            )

        @pl.loop(1, dp)
        def _(i):
            pl.semaphore_signal(
                barrier, inc=1, device_id=(lax.rem(me_dp + i, dp), me), device_id_type=MESH
            )

        for q in range(chunks):
            wsend[q, :, 0:width] = w_in[:, q * width : (q + 1) * width]
            wsend[q, :, width : 2 * width] = w_in[
                :, channels + q * width : channels + (q + 1) * width
            ]

        pair_chunk = me_dp // cc
        pair_row = lax.rem(me_dp, cc)
        for part in range(2):
            begin = pl.multiple_of((2 * pair_chunk + part) * width, width)
            for j in range(QUARTER):
                ftmp[j] = filt[j * lanes : (j + 1) * lanes, pl.ds(begin, width)].T
            for j in range(QUARTER):
                ffs[pl.ds(part * QUARTER + j, seq, stride=2 * QUARTER), :] = ftmp[
                    j, pl.ds(pl.multiple_of(pair_row * seq, seq), seq), :
                ]

        pl.semaphore_wait(barrier, seq - 1 + dp - 1)

        def send_weights(q):
            pltpu.make_async_copy(
                wsend.at[q], wall.at[q, pl.ds(me_dp * dp_rows, dp_rows), :], w_r.at[q]
            ).start()

            @pl.loop(1, dp)
            def _(i):
                remote(
                    wsend.at[q],
                    wall.at[q, pl.ds(me_dp * dp_rows, dp_rows), :],
                    w_s.at[q], w_r.at[q], lax.rem(me_dp + i, dp), me,
                ).start()

        send_weights(0)
        eight = 2 * QUARTER
        pltpu.make_async_copy(
            ffs.at[pl.ds(me * eight, eight), :],
            fall.at[me_dp, pl.ds(me * eight, eight), :],
            ff_r,
        ).start()

        @pl.loop(1, seq)
        def _(i):
            target = lax.rem(me + i, seq)
            remote(
                ffs.at[pl.ds(target * eight, eight), :],
                fall.at[me_dp, pl.ds(me * eight, eight), :],
                ff_s, ff_r, me_dp, target,
            ).start()

        @pl.loop(1, chunks)
        def _(q):
            send_weights(q)

        token_values = tok[0]
        high, low = split(token_values)
        th[...] = high
        tl[...] = low
        for j in range(QUARTER):
            for k in range(chunks):
                block = tok[0, j * lanes : (j + 1) * lanes, k * width : (k + 1) * width].T
                high, low = split(block)
                tth[k * width : (k + 1) * width, j * lanes : (j + 1) * lanes] = high
                ttl[k * width : (k + 1) * width, j * lanes : (j + 1) * lanes] = low

        wait_bytes(fall.at[me_dp], ff_r)

        @pl.loop(1, dp)
        def _(i):
            remote(
                fall.at[me_dp], fall.at[me_dp], fg_s, fg_r, lax.rem(me_dp + i, dp), me
            ).start()

        def exchange(source, target_ref, q, send, recv):
            pltpu.make_async_copy(
                source.at[q, :, pl.ds(me * eight, eight), :],
                target_ref.at[q, :, pl.ds(me * eight, eight), :],
                recv.at[q],
            ).start()

            @pl.loop(1, seq)
            def _(i):
                target = lax.rem(me + i, seq)
                remote(
                    source.at[q, :, pl.ds(target * eight, eight), :],
                    target_ref.at[q, :, pl.ds(me * eight, eight), :],
                    send.at[q], recv.at[q], me_dp, target,
                ).start()

        @pl.loop(0, chunks)
        def _(q):
            wait_bytes(wall.at[q], w_r.at[q])
            w_high, w_low = split(wall[q])
            wh[q] = w_high
            wl[q] = w_low
            projected = dot3((th[...], tl[...]), (w_high, w_low))
            gates = projected[:, width:]
            gate[q] = gates
            conv_grad = cot[0, :, pl.ds(pl.multiple_of(q * width, width), width)] * gates
            for part, values in ((0, projected[:, :width]), (1, conv_grad)):
                for j in range(QUARTER):
                    turned = values[j * lanes : (j + 1) * lanes].T
                    for c in range(cc):
                        fsend[q, c, pl.ds(part * QUARTER + j, seq, stride=eight), :] = turned[
                            c * seq : (c + 1) * seq
                        ]
            exchange(fsend, frecv, q, fs, fr)

        cos_t = ct[...]
        sin_t = st[...]

        def columns(blocks):
            return jnp.concatenate(blocks, axis=1)

        def forward_first(blocks):
            out = dot3((f1h[...], f1l[...]), split(columns(blocks)))
            parts = []
            for c in range(cc):
                lane = out[:, c * lanes : (c + 1) * lanes]
                parts.append([lane[k * n1 : (k + 1) * n1] for k in range(4)])
            return parts

        wait_bytes(fall.at[0 : dp - 1], fg_r)

        @pl.loop(0, chunks // 2)
        def _(p):
            parts = forward_first([fall[p * cc + c] for c in range(cc)])
            for part in range(2):
                stacked = []
                for c in range(cc):
                    real, imag = parts[c][2 * part], parts[c][2 * part + 1]
                    if part == 1:
                        imag = -imag
                    stacked.append(
                        columns([real * cos_t + imag * sin_t, imag * cos_t - real * sin_t])
                    )
                spec[2 * p + part] = dot3(
                    split(jnp.concatenate(stacked, axis=0)), (g2h[...], g2l[...])
                )

        @pl.loop(0, chunks)
        def _(q):
            wait_bytes(frecv.at[q], fr.at[q])
            parts = forward_first([frecv[q, c] for c in range(cc)])
            re_in, im_in = [], []
            for c in range(cc):
                a, b, e, f = parts[c]
                a, b = a * cos_t + b * sin_t, b * cos_t - a * sin_t
                e, f = e * cos_t - f * sin_t, f * cos_t + e * sin_t
                re_in.append(columns([a - f, b - e]))
                im_in.append(columns([b + e, a + f]))
            real = dot3(split(jnp.concatenate(re_in, axis=0)), (frh[...], frl[...]))
            imag = dot3(split(jnp.concatenate(im_in, axis=0)), (fih[...], fil[...]))
            h_real = spec[q, :, :lanes]
            h_imag = spec[q, :, lanes:]
            product = columns([real * h_real - imag * h_imag, real * h_imag + imag * h_real])
            inner = dot3(split(product), (i2h[...], i2l[...]))
            out_in = []
            for c in range(cc):
                block = inner[c * n1 : (c + 1) * n1]
                g, h, g2, h2 = [block[:, k * lanes : (k + 1) * lanes] for k in range(4)]
                out_in.append(
                    jnp.concatenate(
                        [
                            g * cos_t - h * sin_t,
                            h * cos_t + g * sin_t,
                            g2 * cos_t + h2 * sin_t,
                            h2 * cos_t - g2 * sin_t,
                        ],
                        axis=0,
                    )
                )
            result = dot3((i1h[...], i1l[...]), split(columns(out_in)))
            for c in range(cc):
                bsend[q, c] = result[:, c * lanes : (c + 1) * lanes]
            exchange(bsend, brecv, q, bs, br)

        def reduce_dp(q):
            wait_bytes(sib.at[q], sib_r.at[q])
            total = wg[q, :, core] + sib[q]
            rsend[q] = total
            pltpu.make_async_copy(rsend.at[q, me_dp], rrecv.at[q, me_dp], rs_r.at[q]).start()

            @pl.loop(1, dp)
            def _(i):
                target = lax.rem(me_dp + i, dp)
                remote(
                    rsend.at[q, target], rrecv.at[q, me_dp],
                    rs_s.at[q], rs_r.at[q], target, me,
                ).start()

        def sum_dp(q):
            wait_bytes(rrecv.at[q], rs_r.at[q])
            total = rrecv[q, 0]
            for k in range(1, dp):
                total = total + rrecv[q, k]
            rsum[pl.ds(q * groups, groups)] = total.reshape(groups, piece, 2 * width)

        @pl.loop(0, chunks)
        def _(q):
            wait_bytes(brecv.at[q], br.at[q])
            results = []
            for part in range(2):
                blocks = []
                for j in range(QUARTER):
                    turned = jnp.concatenate(
                        [
                            brecv[q, c, pl.ds(part * QUARTER + j, seq, stride=eight), :]
                            for c in range(cc)
                        ],
                        axis=0,
                    )
                    blocks.append(turned.T)
                results.append(jnp.concatenate(blocks, axis=0))
            convolved, d_value = results
            lane = pl.ds(pl.multiple_of(q * width, width), width)
            mixed[0, :, lane] = gate[q] * convolved
            d_pre = split(columns([d_value, cot[0, :, lane] * convolved]))
            grad = dot3((tth[...], ttl[...]), d_pre)
            wg[q] = grad.reshape(dp, CORES, half_rows, 2 * width)
            remote(
                wg.at[q, :, CORES - 1 - core], sib.at[q],
                sib_s.at[q], sib_r.at[q], me_dp, sibling,
            ).start()
            back = dot3(d_pre, (wh[q], wl[q]), ((1,), (1,)))

            @pl.when(q == 0)
            def _():
                token_grad[0] = back

            @pl.when(q > 0)
            def _():
                token_grad[0] = token_grad[0] + back

            reduce_dp(q)

        @pl.loop(0, chunks)
        def _(q):
            sum_dp(q)

        pltpu.make_async_copy(rsum.at[chip], precv.at[chip], p_r).start()

        @pl.loop(1, chips)
        def _(i):
            target = lax.rem(chip + i, chips)
            remote(
                rsum.at[target], precv.at[chip], p_s, p_r, me_dp, target * CORES + core
            ).start()

        wait_bytes(precv, p_r)
        total = precv[0]
        for k in range(1, chips):
            total = total + precv[k]
        agsend[...] = total * scale
        pltpu.make_async_copy(agsend, agrecv.at[me], ag_r).start()

        @pl.loop(1, seq)
        def _(i):
            remote(agsend, agrecv.at[me], ag_s, ag_r, me_dp, lax.rem(me + i, seq)).start()

        wait_bytes(agrecv, ag_r)
        for s in range(seq):
            q, g = (s // CORES) // groups, (s // CORES) % groups
            row = (s % CORES) * half_rows + g * piece
            got = agrecv[s]
            weight_grad[row : row + piece, q * width : (q + 1) * width] = got[:, :width]
            weight_grad[
                row : row + piece, channels + q * width : channels + (q + 1) * width
            ] = got[:, width:]

        @pl.loop(0, chunks)
        def _(q):
            wait_bytes(wall.at[q, 0 : (dp - 1) * dp_rows, :], w_s.at[q])
            wait_bytes(fsend.at[q, :, 0 : (seq - 1) * eight, :], fs.at[q])
            wait_bytes(bsend.at[q, :, 0 : (seq - 1) * eight, :], bs.at[q])
            wait_bytes(sib.at[q], sib_s.at[q])
            wait_bytes(rsend.at[q, 0 : dp - 1], rs_s.at[q])

        wait_bytes(ffs.at[0 : (seq - 1) * eight, :], ff_s)
        wait_bytes(fall.at[0 : dp - 1], fg_s)
        wait_bytes(rsum.at[0 : chips - 1], p_s)
        wait_bytes(agrecv.at[0 : seq - 1], ag_s)

    dma = pltpu.SemaphoreType.DMA
    f32, bf16 = F32, BF16
    scratch = [
        pltpu.VMEM((chunks, dp_rows, 2 * width), f32),
        pltpu.VMEM((chunks, channels, 2 * width), f32),
        pltpu.VMEM((chunks, channels, 2 * width), bf16),
        pltpu.VMEM((chunks, channels, 2 * width), bf16),
        pltpu.VMEM((rows, channels), bf16),
        pltpu.VMEM((rows, channels), bf16),
        pltpu.VMEM((channels, rows), bf16),
        pltpu.VMEM((channels, rows), bf16),
        pltpu.VMEM((chunks, rows, width), f32),
        pltpu.VMEM((chunks, cc, 2 * n1, lanes), f32),
        pltpu.VMEM((chunks, cc, 2 * n1, lanes), f32),
        pltpu.VMEM((chunks, cc, 2 * n1, lanes), f32),
        pltpu.VMEM((chunks, cc, 2 * n1, lanes), f32),
        pltpu.VMEM((QUARTER, width, lanes), f32),
        pltpu.VMEM((2 * n1, lanes), f32),
        pltpu.VMEM((dp, 2 * n1, lanes), f32),
        pltpu.VMEM((chunks, cc * n1, 2 * lanes), f32),
        pltpu.VMEM((chunks, dp, CORES, half_rows, 2 * width), f32),
        pltpu.VMEM((chunks, dp, half_rows, 2 * width), f32),
        pltpu.VMEM((chunks, dp, half_rows, 2 * width), f32),
        pltpu.VMEM((chunks, dp, half_rows, 2 * width), f32),
        pltpu.VMEM((chips, piece, 2 * width), f32),
        pltpu.VMEM((chips, piece, 2 * width), f32),
        pltpu.VMEM((piece, 2 * width), f32),
        pltpu.VMEM((seq, piece, 2 * width), f32),
        dma((chunks,)), dma((chunks,)), dma, dma, dma, dma,
        dma((chunks,)), dma((chunks,)), dma((chunks,)), dma((chunks,)),
        dma((chunks,)), dma((chunks,)), dma((chunks,)), dma((chunks,)),
        dma, dma, dma, dma,
    ]
    return kernel, scratch


def shards(dp, seq, tokens, in_weight, filters, cotangent):
    _, rows, channels = tokens.shape
    lanes = rows // QUARTER
    constants = tables(seq, lanes)
    kernel, scratch = build_kernel(dp, seq, channels, lanes, dp * seq * rows)
    whole = pl.BlockSpec(memory_space=pltpu.VMEM)
    return pl.pallas_call(
        kernel,
        out_shape=(
            jax.ShapeDtypeStruct(tokens.shape, F32),
            jax.ShapeDtypeStruct(tokens.shape, F32),
            jax.ShapeDtypeStruct(in_weight.shape, F32),
        ),
        in_specs=[whole] * (4 + len(constants)),
        out_specs=(whole,) * 3,
        scratch_shapes=scratch,
        compiler_params=pltpu.CompilerParams(
            collective_id=0, has_side_effects=True, vmem_limit_bytes=60 * 1024 * 1024
        ),
        name="gated_conv_layer",
    )(tokens, in_weight, filters, cotangent, *[jnp.asarray(c) for c in constants])


def solution(mesh):
    dp, seq = mesh.shape["dp"], mesh.shape["seq"]

    def local(tokens, in_weight, filters, cotangent):
        return shards(dp, seq, tokens, in_weight, filters, cotangent)

    placed = (P("dp", "seq", None), P("dp", None), P("seq", None), P("dp", "seq", None))
    return jax.shard_map(
        local,
        mesh=mesh,
        in_specs=placed,
        out_specs=(P("dp", "seq", None), P("dp", "seq", None), P("dp", None)),
        check_vma=False,
    )
```

```python
import math

import jax
import jax.numpy as jnp
import numpy as np
from jax import lax
from jax.experimental import pallas as pl
from jax.experimental.pallas import tpu as pltpu
from jax.sharding import PartitionSpec as P

F32 = jnp.float32
BF16 = jnp.bfloat16
MESH = pl.DeviceIdType.MESH
CORES = 2
QUARTER = 4
FILTER_SEND = 1
FILTER_FORWARD = 2
CHUNK_CHANNELS = 4


def split_np(values):
    high = values.astype(np.float32).astype(jnp.bfloat16)
    low = (values - high.astype(np.float64)).astype(np.float32).astype(jnp.bfloat16)
    return high, low


def trig(rows, columns, period):
    product = np.outer(np.arange(rows), np.arange(columns)) % period
    angle = 2.0 * np.pi * product / period
    return np.cos(angle), np.sin(angle)


def tables(seq, lanes):
    n1 = QUARTER * seq
    total = n1 * lanes
    c1, s1 = trig(n1, n1, n1)
    c2, s2 = trig(lanes, lanes, lanes)
    ct, st = trig(n1, lanes, total)
    n1_of = np.arange(n1).reshape(seq, QUARTER)
    zeros = np.zeros((n1, seq, QUARTER))
    top_v = np.concatenate([c1[:, n1_of], zeros], axis=2).reshape(n1, 2 * n1)
    bot_v = np.concatenate([-s1[:, n1_of], zeros], axis=2).reshape(n1, 2 * n1)
    top_d = np.concatenate([zeros, c1[:, n1_of]], axis=2).reshape(n1, 2 * n1)
    bot_d = np.concatenate([zeros, s1[:, n1_of]], axis=2).reshape(n1, 2 * n1)
    forward1 = np.concatenate([top_v, bot_v, top_d, bot_d], axis=0)
    forward_re = np.concatenate([c2, s2], axis=0)
    forward_im = np.concatenate([c2, -s2], axis=0)
    filter2 = np.block([[c2, -s2], [s2, c2]])
    inverse2 = np.block([[c2, s2, c2, -s2], [-s2, c2, s2, c2]])
    zero = np.zeros((n1, n1))
    conv_rows = np.concatenate([c1, -s1, zero, zero], axis=1) / total
    value_rows = np.concatenate([zero, zero, -s1, c1], axis=1) / total
    inverse1 = np.stack(
        [conv_rows.reshape(seq, QUARTER, 4 * n1), value_rows.reshape(seq, QUARTER, 4 * n1)],
        axis=1,
    ).reshape(2 * n1, 4 * n1)
    halves = [
        part
        for matrix in (forward1, forward_re, forward_im, filter2, inverse2, inverse1)
        for part in split_np(matrix)
    ]
    return halves + [ct.astype(np.float32), st.astype(np.float32)]


def split(values):
    high = values.astype(BF16)
    return high, (values - high.astype(F32)).astype(BF16)


def dot3(a, b, dims=((1,), (0,))):
    def one(x, y):
        return lax.dot_general(x, y, (dims, ((), ())), preferred_element_type=F32)

    return one(a[0], b[0]) + one(a[0], b[1]) + one(a[1], b[0])


def build_kernel(dp, seq, channels, lanes, token_total, table_shapes):
    cc = CHUNK_CHANNELS
    width = cc * seq
    chunks = channels // width
    rows = QUARTER * lanes
    n1 = QUARTER * seq
    dp_rows = channels // dp
    half_rows = dp_rows // CORES
    chips = seq // CORES
    rounds = chunks // 2
    groups = chips // 4
    piece = half_rows // groups
    assert rounds * cc == dp and groups * 4 == chips and piece * groups == half_rows
    scale = 1.0 / math.sqrt(token_total)

    def kernel(
        tok_hbm, w_hbm, filt_hbm, cot_hbm,
        f1h_x, f1l_x, frh_x, frl_x, fih_x, fil_x, g2h_x, g2l_x,
        i2h_x, i2l_x, i1h_x, i1l_x, ct_x, st_x,
        mixed_hbm, token_grad_hbm, weight_grad_hbm,
        f1h, f1l, frh, frl, fih, fil, g2h, g2l, i2h, i2l, i1h, i1l, ct, st,
        tok, w_in, filt, cot, mixed, token_grad, weight_grad,
        wall, wh, wl, th, tl, tth, ttl, gate,
        fsend, frecv, bsend, brecv,
        ftmp, ffs, fall, spec,
        wg, sib, rsend, rrecv, rsum, precv, agsend, agrecv,
        in_s, table_s, mixed_s, out_s,
        wy_s, wy_r, wx_s, wx_r, wc_s, wc_r, ff_s, ff_r, fy_s, fy_r, fg_s, fg_r, fs, fr, bs, br,
        sib_s, sib_r, rs_s, rs_r, p_s, p_r, ag_s, ag_r,
    ):
        me_dp = lax.axis_index("dp")
        me = lax.axis_index("seq")
        core = lax.rem(me, CORES)
        chip = me // CORES
        other = CORES - 1 - core
        sibling = chip * CORES + other
        column = me_dp // 2
        row = lax.rem(me_dp, 2)
        partner = column * 2 + 1 - row

        def remote(src, dst, send, recv, d, s):
            return pltpu.make_async_remote_copy(
                src_ref=src, dst_ref=dst, send_sem=send, recv_sem=recv,
                device_id=(d, s), device_id_type=MESH,
            )

        def wait_bytes(ref, sem):
            pltpu.make_async_copy(ref, ref, sem).wait()

        pair_chunk = me_dp // cc
        pair_row = lax.rem(me_dp, cc)
        begin = pl.multiple_of(2 * pair_chunk * width, width)
        inputs = [
            pltpu.make_async_copy(w_hbm, w_in, in_s.at[0]),
            pltpu.make_async_copy(filt_hbm.at[:, pl.ds(begin, 2 * width)], filt, in_s.at[1]),
            pltpu.make_async_copy(tok_hbm.at[0], tok, in_s.at[2]),
            pltpu.make_async_copy(cot_hbm.at[0], cot, in_s.at[3]),
        ]
        sources = [
            f1h_x, f1l_x, frh_x, frl_x, fih_x, fil_x, g2h_x, g2l_x,
            i2h_x, i2l_x, i1h_x, i1l_x, ct_x, st_x,
        ]
        targets = [f1h, f1l, frh, frl, fih, fil, g2h, g2l, i2h, i2l, i1h, i1l, ct, st]
        constants = [
            pltpu.make_async_copy(source, target, table_s.at[k])
            for k, (source, target) in enumerate(zip(sources, targets))
        ]
        for copy in inputs + constants:
            copy.start()

        barrier = pltpu.get_barrier_semaphore()

        @pl.loop(1, seq)
        def _(i):
            pl.semaphore_signal(
                barrier, inc=1, device_id=(me_dp, lax.rem(me + i, seq)), device_id_type=MESH
            )

        @pl.loop(1, dp)
        def _(i):
            pl.semaphore_signal(
                barrier, inc=1, device_id=(lax.rem(me_dp + i, dp), me), device_id_type=MESH
            )

        inputs[0].wait()
        for q in range(chunks):
            for h in range(2):
                begin = h * channels + q * width
                wall[q, me_dp, core, :, h * width : (h + 1) * width] = w_in[
                    pl.ds(pl.multiple_of(core * half_rows, 8), half_rows), begin : begin + width
                ]

        pl.semaphore_wait(barrier, seq - 1 + dp - 1)

        def send_along(block, send, recv):
            @pl.loop(1, dp // 2)
            def _(i):
                target = lax.rem(column + i, dp // 2) * 2 + row
                remote(block, block, send, recv, target, me).start()

        def weights_pair(q):
            block = wall.at[q, me_dp, core]
            remote(block, block, wy_s.at[q], wy_r.at[q], partner, me).start()

        def weights_own(q):
            send_along(wall.at[q, me_dp, core], wx_s.at[q], wx_r.at[q])

        def weights_forward(q):
            block = wall.at[q, partner, core]
            wait_bytes(block, wy_r.at[q])
            send_along(block, wx_s.at[q], wx_r.at[q])

        def weights_share(q):
            wait_bytes(wall.at[q, 0 : dp - 2, 0], wx_r.at[q])
            block = wall.at[q, :, core]
            remote(block, block, wc_s.at[q], wc_r.at[q], me_dp, sibling).start()

        weights_pair(0)
        weights_own(0)

        @pl.loop(1, chunks)
        def _(q):
            weights_pair(q)

        inputs[1].wait()
        for part in range(2):
            for j in range(QUARTER):
                ftmp[j] = filt[
                    j * lanes : (j + 1) * lanes, part * width : (part + 1) * width
                ].T
            for j in range(QUARTER):
                ffs[pl.ds(part * QUARTER + j, seq, stride=2 * QUARTER), :] = ftmp[
                    j, pl.ds(pl.multiple_of(pair_row * seq, seq), seq), :
                ]

        weights_forward(0)
        weights_own(1)
        weights_forward(1)
        eight = 2 * QUARTER
        pltpu.make_async_copy(
            ffs.at[pl.ds(me * eight, eight), :],
            fall.at[me_dp, pl.ds(me * eight, eight), :],
            ff_r,
        ).start()

        @pl.loop(1, seq)
        def _(i):
            target = lax.rem(me + i, seq)
            remote(
                ffs.at[pl.ds(target * eight, eight), :],
                fall.at[me_dp, pl.ds(me * eight, eight), :],
                ff_s, ff_r, me_dp, target,
            ).start()

        inputs[2].wait()
        high, low = split(tok[...])
        th[...] = high
        tl[...] = low
        inputs[3].wait()
        weights_share(0)

        def exchange(source, target_ref, q, send, recv):
            pltpu.make_async_copy(
                source.at[q, :, pl.ds(me * eight, eight), :],
                target_ref.at[q, :, pl.ds(me * eight, eight), :],
                recv.at[q],
            ).start()

            @pl.loop(1, seq)
            def _(i):
                target = lax.rem(me + i, seq)
                remote(
                    source.at[q, :, pl.ds(target * eight, eight), :],
                    target_ref.at[q, :, pl.ds(me * eight, eight), :],
                    send.at[q], recv.at[q], me_dp, target,
                ).start()

        @pl.loop(0, chunks)
        def _(q):
            wait_bytes(wall.at[q, :, other], wc_r.at[q])
            w_high, w_low = split(wall[q].reshape(channels, 2 * width))
            wh[q] = w_high
            wl[q] = w_low
            projected = dot3((th[...], tl[...]), (w_high, w_low))
            gates = projected[:, width:]
            gate[q] = gates
            conv_grad = cot[:, pl.ds(pl.multiple_of(q * width, width), width)] * gates
            for part, values in ((0, projected[:, :width]), (1, conv_grad)):
                for j in range(QUARTER):
                    turned = values[j * lanes : (j + 1) * lanes].T
                    for c in range(cc):
                        fsend[q, c, pl.ds(part * QUARTER + j, seq, stride=eight), :] = turned[
                            c * seq : (c + 1) * seq
                        ]

            @pl.when(q < chunks - 1)
            def _():
                weights_share(q + 1)

            @pl.when(q < chunks - 2)
            def _():
                weights_own(q + 2)
                weights_forward(q + 2)

            @pl.when(q == FILTER_SEND)
            def _():
                wait_bytes(fall.at[me_dp], ff_r)
                block = fall.at[me_dp]
                remote(block, block, fy_s, fy_r, partner, me).start()
                send_along(block, fg_s, fg_r)

            @pl.when(q == FILTER_FORWARD)
            def _():
                wait_bytes(fall.at[partner], fy_r)
                send_along(fall.at[partner], fg_s, fg_r)

            exchange(fsend, frecv, q, fs, fr)

        for j in range(QUARTER):
            for k in range(chunks):
                block = tok[j * lanes : (j + 1) * lanes, k * width : (k + 1) * width].T
                high, low = split(block)
                tth[k * width : (k + 1) * width, j * lanes : (j + 1) * lanes] = high
                ttl[k * width : (k + 1) * width, j * lanes : (j + 1) * lanes] = low

        for copy in constants:
            copy.wait()
        cos_t = ct[...]
        sin_t = st[...]

        def columns(blocks):
            return jnp.concatenate(blocks, axis=1)

        def forward_first(blocks):
            out = dot3((f1h[...], f1l[...]), split(columns(blocks)))
            parts = []
            for c in range(cc):
                lane = out[:, c * lanes : (c + 1) * lanes]
                parts.append([lane[k * n1 : (k + 1) * n1] for k in range(4)])
            return parts

        wait_bytes(fall.at[0 : dp - 2], fg_r)

        @pl.loop(0, chunks // 2)
        def _(p):
            parts = forward_first([fall[p * cc + c] for c in range(cc)])
            for part in range(2):
                stacked = []
                for c in range(cc):
                    real, imag = parts[c][2 * part], parts[c][2 * part + 1]
                    if part == 1:
                        imag = -imag
                    stacked.append(
                        columns([real * cos_t + imag * sin_t, imag * cos_t - real * sin_t])
                    )
                spec[2 * p + part] = dot3(
                    split(jnp.concatenate(stacked, axis=0)), (g2h[...], g2l[...])
                )

        @pl.loop(0, chunks)
        def _(q):
            wait_bytes(frecv.at[q], fr.at[q])
            parts = forward_first([frecv[q, c] for c in range(cc)])
            re_in, im_in = [], []
            for c in range(cc):
                a, b, e, f = parts[c]
                a, b = a * cos_t + b * sin_t, b * cos_t - a * sin_t
                e, f = e * cos_t - f * sin_t, f * cos_t + e * sin_t
                re_in.append(columns([a - f, b - e]))
                im_in.append(columns([b + e, a + f]))
            real = dot3(split(jnp.concatenate(re_in, axis=0)), (frh[...], frl[...]))
            imag = dot3(split(jnp.concatenate(im_in, axis=0)), (fih[...], fil[...]))
            h_real = spec[q, :, :lanes]
            h_imag = spec[q, :, lanes:]
            product = columns([real * h_real - imag * h_imag, real * h_imag + imag * h_real])
            inner = dot3(split(product), (i2h[...], i2l[...]))
            out_in = []
            for c in range(cc):
                block = inner[c * n1 : (c + 1) * n1]
                g, h, g2, h2 = [block[:, k * lanes : (k + 1) * lanes] for k in range(4)]
                out_in.append(
                    jnp.concatenate(
                        [
                            g * cos_t - h * sin_t,
                            h * cos_t + g * sin_t,
                            g2 * cos_t + h2 * sin_t,
                            h2 * cos_t - g2 * sin_t,
                        ],
                        axis=0,
                    )
                )
            result = dot3((i1h[...], i1l[...]), split(columns(out_in)))
            for c in range(cc):
                bsend[q, c] = result[:, c * lanes : (c + 1) * lanes]

            @pl.when(q < 2)
            def _():
                exchange(bsend, brecv, q, bs, br)

        def reduce_dp(q):
            wait_bytes(sib.at[q], sib_r.at[q])
            total = wg[q, :, core] + sib[q]
            rsend[q] = total
            pltpu.make_async_copy(rsend.at[q, me_dp], rrecv.at[q, me_dp], rs_r.at[q]).start()

            @pl.loop(1, dp)
            def _(i):
                target = lax.rem(me_dp + i, dp)
                remote(
                    rsend.at[q, target], rrecv.at[q, me_dp],
                    rs_s.at[q], rs_r.at[q], target, me,
                ).start()

        def sum_dp(q):
            wait_bytes(rrecv.at[q], rs_r.at[q])
            total = rrecv[q, 0]
            for k in range(1, dp):
                total = total + rrecv[q, k]
            for g in range(groups):
                for h in range(2):
                    rsum[q // 2, lax.rem(q, 2) * 2 * groups + 2 * g + h] = total[
                        g * piece : (g + 1) * piece, h * width : (h + 1) * width
                    ]

        def scatter_seq(r):
            pltpu.make_async_copy(rsum.at[r, chip], precv.at[r, chip], p_r.at[r]).start()

            @pl.loop(1, chips)
            def _(i):
                target = lax.rem(chip + i, chips)
                remote(
                    rsum.at[r, target], precv.at[r, chip],
                    p_s.at[r], p_r.at[r], me_dp, target * CORES + core,
                ).start()

        def gather_seq(r):
            wait_bytes(precv.at[r], p_r.at[r])
            total = precv[r, 0]
            for k in range(1, chips):
                total = total + precv[r, k]
            agsend[r] = total * scale
            pltpu.make_async_copy(agsend.at[r], agrecv.at[r, me], ag_r.at[r]).start()

            @pl.loop(1, seq)
            def _(i):
                remote(
                    agsend.at[r], agrecv.at[r, me],
                    ag_s.at[r], ag_r.at[r], me_dp, lax.rem(me + i, seq),
                ).start()

        @pl.loop(0, chunks)
        def _(q):
            wait_bytes(brecv.at[q], br.at[q])
            results = []
            for part in range(2):
                blocks = []
                for j in range(QUARTER):
                    turned = jnp.concatenate(
                        [
                            brecv[q, c, pl.ds(part * QUARTER + j, seq, stride=eight), :]
                            for c in range(cc)
                        ],
                        axis=0,
                    )
                    blocks.append(turned.T)
                results.append(jnp.concatenate(blocks, axis=0))
            convolved, d_value = results
            lane = pl.ds(pl.multiple_of(q * width, width), width)
            d_pre = split(columns([d_value, cot[:, lane] * convolved]))
            grad = dot3((tth[...], ttl[...]), d_pre)
            wg[q] = grad.reshape(dp, CORES, half_rows, 2 * width)
            remote(
                wg.at[q, :, CORES - 1 - core], sib.at[q],
                sib_s.at[q], sib_r.at[q], me_dp, sibling,
            ).start()

            @pl.when(q > 0)
            def _():
                reduce_dp(q - 1)

            @pl.when(q < chunks - 2)
            def _():
                exchange(bsend, brecv, q + 2, bs, br)

            mixed[q] = gate[q] * convolved
            pltpu.make_async_copy(mixed.at[q], mixed_hbm.at[0, :, lane], mixed_s.at[q]).start()
            back = dot3(d_pre, (wh[q], wl[q]), ((1,), (1,)))

            @pl.when(q == 0)
            def _():
                token_grad[...] = back

            @pl.when(q > 0)
            def _():
                token_grad[...] = token_grad[...] + back

        grad_copy = pltpu.make_async_copy(token_grad, token_grad_hbm.at[0], out_s.at[0])
        grad_copy.start()
        for r in range(rounds - 1):
            sum_dp(2 * r)
            sum_dp(2 * r + 1)
            scatter_seq(r)
        reduce_dp(chunks - 1)
        for r in range(rounds - 1):
            gather_seq(r)
        sum_dp(chunks - 2)
        sum_dp(chunks - 1)
        scatter_seq(rounds - 1)
        gather_seq(rounds - 1)
        for r in range(rounds):
            wait_bytes(agrecv.at[r], ag_r.at[r])
            for s in range(seq):
                p = s // CORES
                q, g, h = 2 * r + p // (2 * groups), (p % (2 * groups)) // 2, p % 2
                row = (s % CORES) * half_rows + g * piece
                column = h * channels + q * width
                weight_grad[row : row + piece, column : column + width] = agrecv[r, s]
        weight_copy = pltpu.make_async_copy(weight_grad, weight_grad_hbm, out_s.at[1])
        weight_copy.start()

        @pl.loop(0, chunks)
        def _(q):
            wait_bytes(wall.at[q, 0, 0], wy_s.at[q])
            wait_bytes(wall.at[q, 0 : dp - 2, 0], wx_s.at[q])
            wait_bytes(wall.at[q, :, 0], wc_s.at[q])
            wait_bytes(fsend.at[q, :, 0 : (seq - 1) * eight, :], fs.at[q])
            wait_bytes(bsend.at[q, :, 0 : (seq - 1) * eight, :], bs.at[q])
            wait_bytes(sib.at[q], sib_s.at[q])
            wait_bytes(rsend.at[q, 0 : dp - 1], rs_s.at[q])

        wait_bytes(ffs.at[0 : (seq - 1) * eight, :], ff_s)
        wait_bytes(fall.at[0], fy_s)
        wait_bytes(fall.at[0 : dp - 2], fg_s)
        for r in range(rounds):
            wait_bytes(rsum.at[r, 0 : chips - 1], p_s.at[r])
            wait_bytes(agrecv.at[r, 0 : seq - 1], ag_s.at[r])

        @pl.loop(0, chunks)
        def _(q):
            lane = pl.ds(pl.multiple_of(q * width, width), width)
            pltpu.make_async_copy(mixed.at[q], mixed_hbm.at[0, :, lane], mixed_s.at[q]).wait()

        grad_copy.wait()
        weight_copy.wait()

    dma = pltpu.SemaphoreType.DMA
    f32, bf16 = F32, BF16
    scratch = [pltpu.VMEM(shape, kind) for shape, kind in table_shapes] + [
        pltpu.VMEM((rows, channels), f32),
        pltpu.VMEM((dp_rows, 2 * channels), f32),
        pltpu.VMEM((rows, 2 * width), f32),
        pltpu.VMEM((rows, channels), f32),
        pltpu.VMEM((chunks, rows, width), f32),
        pltpu.VMEM((rows, channels), f32),
        pltpu.VMEM((dp_rows, 2 * channels), f32),
        pltpu.VMEM((chunks, dp, CORES, half_rows, 2 * width), f32),
        pltpu.VMEM((chunks, channels, 2 * width), bf16),
        pltpu.VMEM((chunks, channels, 2 * width), bf16),
        pltpu.VMEM((rows, channels), bf16),
        pltpu.VMEM((rows, channels), bf16),
        pltpu.VMEM((channels, rows), bf16),
        pltpu.VMEM((channels, rows), bf16),
        pltpu.VMEM((chunks, rows, width), f32),
        pltpu.VMEM((chunks, cc, 2 * n1, lanes), f32),
        pltpu.VMEM((chunks, cc, 2 * n1, lanes), f32),
        pltpu.VMEM((chunks, cc, 2 * n1, lanes), f32),
        pltpu.VMEM((chunks, cc, 2 * n1, lanes), f32),
        pltpu.VMEM((QUARTER, width, lanes), f32),
        pltpu.VMEM((2 * n1, lanes), f32),
        pltpu.VMEM((dp, 2 * n1, lanes), f32),
        pltpu.VMEM((chunks, cc * n1, 2 * lanes), f32),
        pltpu.VMEM((chunks, dp, CORES, half_rows, 2 * width), f32),
        pltpu.VMEM((chunks, dp, half_rows, 2 * width), f32),
        pltpu.VMEM((chunks, dp, half_rows, 2 * width), f32),
        pltpu.VMEM((chunks, dp, half_rows, 2 * width), f32),
        pltpu.VMEM((rounds, chips, piece, width), f32),
        pltpu.VMEM((rounds, chips, piece, width), f32),
        pltpu.VMEM((rounds, piece, width), f32),
        pltpu.VMEM((rounds, seq, piece, width), f32),
        dma((4,)), dma((len(table_shapes),)), dma((chunks,)), dma((2,)),
        dma((chunks,)), dma((chunks,)), dma((chunks,)), dma((chunks,)),
        dma((chunks,)), dma((chunks,)), dma, dma, dma, dma, dma, dma,
        dma((chunks,)), dma((chunks,)), dma((chunks,)), dma((chunks,)),
        dma((chunks,)), dma((chunks,)), dma((chunks,)), dma((chunks,)),
        dma((rounds,)), dma((rounds,)), dma((rounds,)), dma((rounds,)),
    ]
    return kernel, scratch


def shards(dp, seq, tokens, in_weight, filters, cotangent):
    _, rows, channels = tokens.shape
    lanes = rows // QUARTER
    constants = tables(seq, lanes)
    kernel, scratch = build_kernel(
        dp, seq, channels, lanes, dp * seq * rows, [(c.shape, c.dtype) for c in constants]
    )
    whole = pl.BlockSpec(memory_space=pl.ANY)
    return pl.pallas_call(
        kernel,
        out_shape=(
            jax.ShapeDtypeStruct(tokens.shape, F32),
            jax.ShapeDtypeStruct(tokens.shape, F32),
            jax.ShapeDtypeStruct(in_weight.shape, F32),
        ),
        in_specs=[whole] * (4 + len(constants)),
        out_specs=(whole,) * 3,
        scratch_shapes=scratch,
        compiler_params=pltpu.CompilerParams(
            collective_id=0, has_side_effects=True, vmem_limit_bytes=60 * 1024 * 1024
        ),
        name="gated_conv_layer",
    )(tokens, in_weight, filters, cotangent, *[jnp.asarray(c) for c in constants])


def solution(mesh):
    dp, seq = mesh.shape["dp"], mesh.shape["seq"]

    def local(tokens, in_weight, filters, cotangent):
        return shards(dp, seq, tokens, in_weight, filters, cotangent)

    placed = (P("dp", "seq", None), P("dp", None), P("seq", None), P("dp", "seq", None))
    return jax.shard_map(
        local,
        mesh=mesh,
        in_specs=placed,
        out_specs=(P("dp", "seq", None), P("dp", "seq", None), P("dp", None)),
        check_vma=False,
    )
```

```python
import math

import jax
import jax.numpy as jnp
import numpy as np
from jax import lax
from jax.experimental import pallas as pl
from jax.experimental.pallas import tpu as pltpu
from jax.sharding import PartitionSpec as P

F32 = jnp.float32
BF16 = jnp.bfloat16
MESH = pl.DeviceIdType.MESH
CORES = 2
QUARTER = 4
FILTER_SEND = 1
FILTER_FORWARD = 2
STEPS = 2
CHUNK_CHANNELS = 4


def split_np(values):
    high = values.astype(np.float32).astype(jnp.bfloat16)
    low = (values - high.astype(np.float64)).astype(np.float32).astype(jnp.bfloat16)
    return high, low


def trig(rows, columns, period):
    product = np.outer(np.arange(rows), np.arange(columns)) % period
    angle = 2.0 * np.pi * product / period
    return np.cos(angle), np.sin(angle)


def tables(seq, lanes):
    n1 = QUARTER * seq
    total = n1 * lanes
    c1, s1 = trig(n1, n1, n1)
    c2, s2 = trig(lanes, lanes, lanes)
    ct, st = trig(n1, lanes, total)
    n1_of = np.arange(n1).reshape(seq, QUARTER)
    zeros = np.zeros((n1, seq, QUARTER))
    top_v = np.concatenate([c1[:, n1_of], zeros], axis=2).reshape(n1, 2 * n1)
    bot_v = np.concatenate([-s1[:, n1_of], zeros], axis=2).reshape(n1, 2 * n1)
    top_d = np.concatenate([zeros, c1[:, n1_of]], axis=2).reshape(n1, 2 * n1)
    bot_d = np.concatenate([zeros, s1[:, n1_of]], axis=2).reshape(n1, 2 * n1)
    forward1 = np.concatenate([top_v, bot_v, top_d, bot_d], axis=0)
    forward_re = np.concatenate([c2, s2], axis=0)
    forward_im = np.concatenate([c2, -s2], axis=0)
    filter2 = np.block([[c2, -s2], [s2, c2]])
    inverse2 = np.block([[c2, s2, c2, -s2], [-s2, c2, s2, c2]])
    zero = np.zeros((n1, n1))
    conv_rows = np.concatenate([c1, -s1, zero, zero], axis=1) / total
    value_rows = np.concatenate([zero, zero, -s1, c1], axis=1) / total
    inverse1 = np.stack(
        [conv_rows.reshape(seq, QUARTER, 4 * n1), value_rows.reshape(seq, QUARTER, 4 * n1)],
        axis=1,
    ).reshape(2 * n1, 4 * n1)
    halves = [
        part
        for matrix in (forward1, forward_re, forward_im, filter2, inverse2, inverse1)
        for part in split_np(matrix)
    ]
    return halves + [ct.astype(np.float32), st.astype(np.float32)]


def split(values):
    high = values.astype(BF16)
    return high, (values - high.astype(F32)).astype(BF16)


def dot3(a, b, dims=((1,), (0,))):
    def one(x, y):
        return lax.dot_general(x, y, (dims, ((), ())), preferred_element_type=F32)

    return one(a[0], b[0]) + one(a[0], b[1]) + one(a[1], b[0])


def build_kernel(dp, seq, channels, lanes, token_total, table_shapes):
    cc = CHUNK_CHANNELS
    width = cc * seq
    chunks = channels // width
    rows = QUARTER * lanes
    n1 = QUARTER * seq
    dp_rows = channels // dp
    half_rows = dp_rows // CORES
    chips = seq // CORES
    rounds = chunks // 2
    groups = chips // 4
    piece = half_rows // groups
    assert rounds * cc == dp and groups * 4 == chips and piece * groups == half_rows
    scale = 1.0 / math.sqrt(token_total)

    def kernel(
        tok_hbm, w_hbm, filt_hbm, cot_hbm,
        f1h_x, f1l_x, frh_x, frl_x, fih_x, fil_x, g2h_x, g2l_x,
        i2h_x, i2l_x, i1h_x, i1l_x, ct_x, st_x,
        mixed_hbm, token_grad_hbm, weight_grad_hbm,
        f1h, f1l, frh, frl, fih, fil, g2h, g2l, i2h, i2l, i1h, i1l, ct, st,
        tok, w_in, filt, cot, mixed, token_grad, weight_grad,
        wall, wh, wl, th, tl, tth, ttl, gate,
        fsend, frecv, bsend, brecv,
        ftmp, ffs, fall, spec,
        wg, sib, rsend, rrecv, rsum, precv, agsend, agrecv,
        in_s, table_s, mixed_s, out_s,
        wy_s, wy_r, wx_s, wx_r, wc_s, wc_r, ff_s, ff_r, fy_s, fy_r, fg_s, fg_r, fs, fr, bs, br,
        sib_s, sib_r, rs_s, rs_r, p_s, p_r, ag_s, ag_r,
    ):
        me_dp = lax.axis_index("dp")
        me = lax.axis_index("seq")
        core = lax.rem(me, CORES)
        chip = me // CORES
        other = CORES - 1 - core
        sibling = chip * CORES + other
        column = me_dp // 2
        row = lax.rem(me_dp, 2)
        partner = column * 2 + 1 - row

        def remote(src, dst, send, recv, d, s):
            return pltpu.make_async_remote_copy(
                src_ref=src, dst_ref=dst, send_sem=send, recv_sem=recv,
                device_id=(d, s), device_id_type=MESH,
            )

        def wait_bytes(ref, sem):
            pltpu.make_async_copy(ref, ref, sem).wait()

        pair_chunk = me_dp // cc
        pair_row = lax.rem(me_dp, cc)
        begin = pl.multiple_of(2 * pair_chunk * width, width)
        inputs = [
            pltpu.make_async_copy(w_hbm, w_in, in_s.at[0]),
            pltpu.make_async_copy(filt_hbm.at[:, pl.ds(begin, 2 * width)], filt, in_s.at[1]),
            pltpu.make_async_copy(tok_hbm.at[0], tok, in_s.at[2]),
            pltpu.make_async_copy(cot_hbm.at[0], cot, in_s.at[3]),
        ]
        sources = [
            f1h_x, f1l_x, frh_x, frl_x, fih_x, fil_x, g2h_x, g2l_x,
            i2h_x, i2l_x, i1h_x, i1l_x, ct_x, st_x,
        ]
        targets = [f1h, f1l, frh, frl, fih, fil, g2h, g2l, i2h, i2l, i1h, i1l, ct, st]
        constants = [
            pltpu.make_async_copy(source, target, table_s.at[k])
            for k, (source, target) in enumerate(zip(sources, targets))
        ]
        for copy in inputs + constants:
            copy.start()

        barrier = pltpu.get_barrier_semaphore()

        @pl.loop(1, seq)
        def _(i):
            pl.semaphore_signal(
                barrier, inc=1, device_id=(me_dp, lax.rem(me + i, seq)), device_id_type=MESH
            )

        @pl.loop(1, dp)
        def _(i):
            pl.semaphore_signal(
                barrier, inc=1, device_id=(lax.rem(me_dp + i, dp), me), device_id_type=MESH
            )

        inputs[0].wait()
        for q in range(chunks):
            for h in range(2):
                begin = h * channels + q * width
                wall[q, me_dp, core, :, h * width : (h + 1) * width] = w_in[
                    pl.ds(pl.multiple_of(core * half_rows, 8), half_rows), begin : begin + width
                ]

        pl.semaphore_wait(barrier, seq - 1 + dp - 1)

        def send_along(block, send, recv):
            @pl.loop(1, dp // 2)
            def _(i):
                target = lax.rem(column + i, dp // 2) * 2 + row
                remote(block, block, send, recv, target, me).start()

        def weights_pair(q):
            block = wall.at[q, me_dp, core]
            remote(block, block, wy_s.at[q], wy_r.at[q], partner, me).start()

        def weights_own(q):
            send_along(wall.at[q, me_dp, core], wx_s.at[q], wx_r.at[q])

        def weights_forward(q):
            block = wall.at[q, partner, core]
            wait_bytes(block, wy_r.at[q])
            send_along(block, wx_s.at[q], wx_r.at[q])

        def weights_share(q):
            wait_bytes(wall.at[q, 0 : dp - 2, 0], wx_r.at[q])
            block = wall.at[q, :, core]
            remote(block, block, wc_s.at[q], wc_r.at[q], me_dp, sibling).start()

        weights_pair(0)
        weights_own(0)

        @pl.loop(1, chunks)
        def _(q):
            weights_pair(q)

        inputs[1].wait()
        for part in range(2):
            for j in range(QUARTER):
                ftmp[j] = filt[
                    j * lanes : (j + 1) * lanes, part * width : (part + 1) * width
                ].T
            for j in range(QUARTER):
                ffs[pl.ds(part * QUARTER + j, seq, stride=2 * QUARTER), :] = ftmp[
                    j, pl.ds(pl.multiple_of(pair_row * seq, seq), seq), :
                ]

        weights_forward(0)
        weights_own(1)
        weights_forward(1)
        eight = 2 * QUARTER
        pltpu.make_async_copy(
            ffs.at[pl.ds(me * eight, eight), :],
            fall.at[me_dp, pl.ds(me * eight, eight), :],
            ff_r,
        ).start()

        @pl.loop(1, seq)
        def _(i):
            target = lax.rem(me + i, seq)
            remote(
                ffs.at[pl.ds(target * eight, eight), :],
                fall.at[me_dp, pl.ds(me * eight, eight), :],
                ff_s, ff_r, me_dp, target,
            ).start()

        inputs[2].wait()
        high, low = split(tok[...])
        th[...] = high
        tl[...] = low
        inputs[3].wait()
        weights_share(0)

        def exchange(source, target_ref, q, send, recv):
            pltpu.make_async_copy(
                source.at[q, :, pl.ds(me * eight, eight), :],
                target_ref.at[q, :, pl.ds(me * eight, eight), :],
                recv.at[q],
            ).start()

            @pl.loop(1, seq)
            def _(i):
                target = lax.rem(me + i, seq)
                remote(
                    source.at[q, :, pl.ds(target * eight, eight), :],
                    target_ref.at[q, :, pl.ds(me * eight, eight), :],
                    send.at[q], recv.at[q], me_dp, target,
                ).start()

        @pl.loop(0, chunks)
        def _(q):
            wait_bytes(wall.at[q, :, other], wc_r.at[q])
            w_high, w_low = split(wall[q].reshape(channels, 2 * width))
            wh[q] = w_high
            wl[q] = w_low
            projected = dot3((th[...], tl[...]), (w_high, w_low))
            gates = projected[:, width:]
            gate[q] = gates
            conv_grad = cot[:, pl.ds(pl.multiple_of(q * width, width), width)] * gates
            for part, values in ((0, projected[:, :width]), (1, conv_grad)):
                for j in range(QUARTER):
                    turned = values[j * lanes : (j + 1) * lanes].T
                    for c in range(cc):
                        fsend[q, c, pl.ds(part * QUARTER + j, seq, stride=eight), :] = turned[
                            c * seq : (c + 1) * seq
                        ]

            @pl.when(q < chunks - 1)
            def _():
                weights_share(q + 1)

            @pl.when(q < chunks - 2)
            def _():
                weights_own(q + 2)
                weights_forward(q + 2)

            @pl.when(q == FILTER_SEND)
            def _():
                wait_bytes(fall.at[me_dp], ff_r)
                block = fall.at[me_dp]
                remote(block, block, fy_s, fy_r, partner, me).start()
                send_along(block, fg_s, fg_r)

            @pl.when(q == FILTER_FORWARD)
            def _():
                wait_bytes(fall.at[partner], fy_r)
                send_along(fall.at[partner], fg_s, fg_r)

            exchange(fsend, frecv, q, fs, fr)

        for j in range(QUARTER):
            for k in range(chunks):
                block = tok[j * lanes : (j + 1) * lanes, k * width : (k + 1) * width].T
                high, low = split(block)
                tth[k * width : (k + 1) * width, j * lanes : (j + 1) * lanes] = high
                ttl[k * width : (k + 1) * width, j * lanes : (j + 1) * lanes] = low

        for copy in constants:
            copy.wait()
        cos_t = ct[...]
        sin_t = st[...]

        def columns(blocks):
            return jnp.concatenate(blocks, axis=1)

        def forward_first(blocks):
            out = dot3((f1h[...], f1l[...]), split(columns(blocks)))
            parts = []
            for c in range(cc):
                lane = out[:, c * lanes : (c + 1) * lanes]
                parts.append([lane[k * n1 : (k + 1) * n1] for k in range(4)])
            return parts

        wait_bytes(fall.at[0 : dp - 2], fg_r)

        @pl.loop(0, chunks // 2)
        def _(p):
            parts = forward_first([fall[p * cc + c] for c in range(cc)])
            for part in range(2):
                stacked = []
                for c in range(cc):
                    real, imag = parts[c][2 * part], parts[c][2 * part + 1]
                    if part == 1:
                        imag = -imag
                    stacked.append(
                        columns([real * cos_t + imag * sin_t, imag * cos_t - real * sin_t])
                    )
                spec[2 * p + part] = dot3(
                    split(jnp.concatenate(stacked, axis=0)), (g2h[...], g2l[...])
                )

        @pl.loop(0, chunks)
        def _(q):
            wait_bytes(frecv.at[q], fr.at[q])
            parts = forward_first([frecv[q, c] for c in range(cc)])
            re_in, im_in = [], []
            for c in range(cc):
                a, b, e, f = parts[c]
                a, b = a * cos_t + b * sin_t, b * cos_t - a * sin_t
                e, f = e * cos_t - f * sin_t, f * cos_t + e * sin_t
                re_in.append(columns([a - f, b - e]))
                im_in.append(columns([b + e, a + f]))
            real = dot3(split(jnp.concatenate(re_in, axis=0)), (frh[...], frl[...]))
            imag = dot3(split(jnp.concatenate(im_in, axis=0)), (fih[...], fil[...]))
            h_real = spec[q, :, :lanes]
            h_imag = spec[q, :, lanes:]
            product = columns([real * h_real - imag * h_imag, real * h_imag + imag * h_real])
            inner = dot3(split(product), (i2h[...], i2l[...]))
            out_in = []
            for c in range(cc):
                block = inner[c * n1 : (c + 1) * n1]
                g, h, g2, h2 = [block[:, k * lanes : (k + 1) * lanes] for k in range(4)]
                out_in.append(
                    jnp.concatenate(
                        [
                            g * cos_t - h * sin_t,
                            h * cos_t + g * sin_t,
                            g2 * cos_t + h2 * sin_t,
                            h2 * cos_t - g2 * sin_t,
                        ],
                        axis=0,
                    )
                )
            result = dot3((i1h[...], i1l[...]), split(columns(out_in)))
            for c in range(cc):
                bsend[q, c] = result[:, c * lanes : (c + 1) * lanes]

            @pl.when(q < 2)
            def _():
                exchange(bsend, brecv, q, bs, br)

        def reduce_dp(q):
            wait_bytes(sib.at[q], sib_r.at[q])
            total = wg[q, :, core] + sib[q]
            rsend[q] = total
            pltpu.make_async_copy(rsend.at[q, me_dp], rrecv.at[q, me_dp], rs_r.at[q]).start()

            @pl.loop(1, dp)
            def _(i):
                target = lax.rem(me_dp + i, dp)
                remote(
                    rsend.at[q, target], rrecv.at[q, me_dp],
                    rs_s.at[q], rs_r.at[q], target, me,
                ).start()

        def sum_dp(q):
            wait_bytes(rrecv.at[q], rs_r.at[q])
            total = rrecv[q, 0]
            for k in range(1, dp):
                total = total + rrecv[q, k]
            for g in range(groups):
                for h in range(2):
                    rsum[q // 2, lax.rem(q, 2) * 2 * groups + 2 * g + h] = total[
                        g * piece : (g + 1) * piece, h * width : (h + 1) * width
                    ]

        def scatter_seq(r):
            pltpu.make_async_copy(rsum.at[r, chip], precv.at[r, chip], p_r.at[r]).start()

            @pl.loop(1, chips)
            def _(i):
                target = lax.rem(chip + i, chips)
                remote(
                    rsum.at[r, target], precv.at[r, chip],
                    p_s.at[r], p_r.at[r], me_dp, target * CORES + core,
                ).start()

        def gather_seq(r):
            wait_bytes(precv.at[r], p_r.at[r])
            total = precv[r, 0]
            for k in range(1, chips):
                total = total + precv[r, k]
            agsend[r] = total * scale
            pltpu.make_async_copy(agsend.at[r], agrecv.at[r, me], ag_r.at[r]).start()

            @pl.loop(1, seq)
            def _(i):
                remote(
                    agsend.at[r], agrecv.at[r, me],
                    ag_s.at[r], ag_r.at[r], me_dp, lax.rem(me + i, seq),
                ).start()

        @pl.loop(0, chunks)
        def _(q):
            wait_bytes(brecv.at[q], br.at[q])
            results = []
            for part in range(2):
                blocks = []
                for j in range(QUARTER):
                    turned = jnp.concatenate(
                        [
                            brecv[q, c, pl.ds(part * QUARTER + j, seq, stride=eight), :]
                            for c in range(cc)
                        ],
                        axis=0,
                    )
                    blocks.append(turned.T)
                results.append(jnp.concatenate(blocks, axis=0))
            convolved, d_value = results
            lane = pl.ds(pl.multiple_of(q * width, width), width)
            d_pre = split(columns([d_value, cot[:, lane] * convolved]))
            grad = dot3((tth[...], ttl[...]), d_pre)
            wg[q] = grad.reshape(dp, CORES, half_rows, 2 * width)
            remote(
                wg.at[q, :, CORES - 1 - core], sib.at[q],
                sib_s.at[q], sib_r.at[q], me_dp, sibling,
            ).start()

            @pl.when(q > 0)
            def _():
                reduce_dp(q - 1)

            @pl.when(q < chunks - 2)
            def _():
                exchange(bsend, brecv, q + 2, bs, br)

            mixed[q] = gate[q] * convolved
            pltpu.make_async_copy(mixed.at[q], mixed_hbm.at[0, :, lane], mixed_s.at[q]).start()
            back = dot3(d_pre, (wh[q], wl[q]), ((1,), (1,)))

            @pl.when(q == 0)
            def _():
                token_grad[...] = back

            @pl.when(q > 0)
            def _():
                token_grad[...] = token_grad[...] + back

        grad_copy = pltpu.make_async_copy(token_grad, token_grad_hbm.at[0], out_s.at[0])
        grad_copy.start()
        reduce_dp(chunks - 1)
        for r in range(rounds):
            sum_dp(2 * r)
            sum_dp(2 * r + 1)
            scatter_seq(r)
        for r in range(rounds):
            gather_seq(r)
        for r in range(rounds):
            wait_bytes(agrecv.at[r], ag_r.at[r])
            for s in range(seq):
                p = s // CORES
                q, g, h = 2 * r + p // (2 * groups), (p % (2 * groups)) // 2, p % 2
                row = (s % CORES) * half_rows + g * piece
                column = h * channels + q * width
                weight_grad[row : row + piece, column : column + width] = agrecv[r, s]
        weight_copy = pltpu.make_async_copy(weight_grad, weight_grad_hbm, out_s.at[1])
        weight_copy.start()

        @pl.loop(0, chunks)
        def _(q):
            wait_bytes(wall.at[q, 0, 0], wy_s.at[q])
            wait_bytes(wall.at[q, 0 : dp - 2, 0], wx_s.at[q])
            wait_bytes(wall.at[q, :, 0], wc_s.at[q])
            wait_bytes(fsend.at[q, :, 0 : (seq - 1) * eight, :], fs.at[q])
            wait_bytes(bsend.at[q, :, 0 : (seq - 1) * eight, :], bs.at[q])
            wait_bytes(sib.at[q], sib_s.at[q])
            wait_bytes(rsend.at[q, 0 : dp - 1], rs_s.at[q])

        wait_bytes(ffs.at[0 : (seq - 1) * eight, :], ff_s)
        wait_bytes(fall.at[0], fy_s)
        wait_bytes(fall.at[0 : dp - 2], fg_s)
        for r in range(rounds):
            wait_bytes(rsum.at[r, 0 : chips - 1], p_s.at[r])
            wait_bytes(agrecv.at[r, 0 : seq - 1], ag_s.at[r])

        @pl.loop(0, chunks)
        def _(q):
            lane = pl.ds(pl.multiple_of(q * width, width), width)
            pltpu.make_async_copy(mixed.at[q], mixed_hbm.at[0, :, lane], mixed_s.at[q]).wait()

        grad_copy.wait()
        weight_copy.wait()

    dma = pltpu.SemaphoreType.DMA
    f32, bf16 = F32, BF16
    scratch = [pltpu.VMEM(shape, kind) for shape, kind in table_shapes] + [
        pltpu.VMEM((rows, channels), f32),
        pltpu.VMEM((dp_rows, 2 * channels), f32),
        pltpu.VMEM((rows, 2 * width), f32),
        pltpu.VMEM((rows, channels), f32),
        pltpu.VMEM((chunks, rows, width), f32),
        pltpu.VMEM((rows, channels), f32),
        pltpu.VMEM((dp_rows, 2 * channels), f32),
        pltpu.VMEM((chunks, dp, CORES, half_rows, 2 * width), f32),
        pltpu.VMEM((chunks, channels, 2 * width), bf16),
        pltpu.VMEM((chunks, channels, 2 * width), bf16),
        pltpu.VMEM((rows, channels), bf16),
        pltpu.VMEM((rows, channels), bf16),
        pltpu.VMEM((channels, rows), bf16),
        pltpu.VMEM((channels, rows), bf16),
        pltpu.VMEM((chunks, rows, width), f32),
        pltpu.VMEM((chunks, cc, 2 * n1, lanes), f32),
        pltpu.VMEM((chunks, cc, 2 * n1, lanes), f32),
        pltpu.VMEM((chunks, cc, 2 * n1, lanes), f32),
        pltpu.VMEM((chunks, cc, 2 * n1, lanes), f32),
        pltpu.VMEM((QUARTER, width, lanes), f32),
        pltpu.VMEM((2 * n1, lanes), f32),
        pltpu.VMEM((dp, 2 * n1, lanes), f32),
        pltpu.VMEM((chunks, cc * n1, 2 * lanes), f32),
        pltpu.VMEM((chunks, dp, CORES, half_rows, 2 * width), f32),
        pltpu.VMEM((chunks, dp, half_rows, 2 * width), f32),
        pltpu.VMEM((chunks, dp, half_rows, 2 * width), f32),
        pltpu.VMEM((chunks, dp, half_rows, 2 * width), f32),
        pltpu.VMEM((rounds, chips, piece, width), f32),
        pltpu.VMEM((rounds, chips, piece, width), f32),
        pltpu.VMEM((rounds, piece, width), f32),
        pltpu.VMEM((rounds, seq, piece, width), f32),
        dma((4,)), dma((len(table_shapes),)), dma((chunks,)), dma((2,)),
        dma((chunks,)), dma((chunks,)), dma((chunks,)), dma((chunks,)),
        dma((chunks,)), dma((chunks,)), dma, dma, dma, dma, dma, dma,
        dma((chunks,)), dma((chunks,)), dma((chunks,)), dma((chunks,)),
        dma((chunks,)), dma((chunks,)), dma((chunks,)), dma((chunks,)),
        dma((rounds,)), dma((rounds,)), dma((rounds,)), dma((rounds,)),
    ]
    return kernel, scratch


def shards(dp, seq, tokens, in_weight, filters, cotangent):
    _, rows, channels = tokens.shape
    lanes = rows // QUARTER
    constants = tables(seq, lanes)
    kernel, scratch = build_kernel(
        dp, seq, channels, lanes, dp * seq * rows, [(c.shape, c.dtype) for c in constants]
    )
    whole = pl.BlockSpec(memory_space=pl.ANY)
    shapes = (
        jax.ShapeDtypeStruct(tokens.shape, F32),
        jax.ShapeDtypeStruct(tokens.shape, F32),
        jax.ShapeDtypeStruct(in_weight.shape, F32),
    )

    def place(a, b, c, x, y, z):
        x[...] = a[...]
        y[...] = b[...]
        z[...] = c[...]

    results = pl.pallas_call(
        kernel,
        out_shape=shapes,
        in_specs=[whole] * (4 + len(constants)),
        out_specs=(whole,) * 3,
        scratch_shapes=scratch,
        compiler_params=pltpu.CompilerParams(
            collective_id=0, has_side_effects=True, vmem_limit_bytes=60 * 1024 * 1024
        ),
        name="gated_conv_layer",
    )(tokens, in_weight, filters, cotangent, *[jnp.asarray(c) for c in constants])
    steps = STEPS
    blocks = (
        pl.BlockSpec((1, rows // steps, channels), lambda i: (0, i, 0)),
        pl.BlockSpec((1, rows // steps, channels), lambda i: (0, i, 0)),
        pl.BlockSpec((in_weight.shape[0] // steps, 2 * channels), lambda i: (i, 0)),
    )
    return pl.pallas_call(
        place,
        grid=(steps,),
        out_shape=shapes,
        in_specs=list(blocks),
        out_specs=blocks,
        name="place_results",
    )(*results)


def solution(mesh):
    dp, seq = mesh.shape["dp"], mesh.shape["seq"]

    def local(tokens, in_weight, filters, cotangent):
        return shards(dp, seq, tokens, in_weight, filters, cotangent)

    placed = (P("dp", "seq", None), P("dp", None), P("seq", None), P("dp", "seq", None))
    return jax.shard_map(
        local,
        mesh=mesh,
        in_specs=placed,
        out_specs=(P("dp", "seq", None), P("dp", "seq", None), P("dp", None)),
        check_vma=False,
    )
```

```python
import math

import jax
import jax.numpy as jnp
import numpy as np
from jax import lax
from jax.experimental import pallas as pl
from jax.experimental.pallas import tpu as pltpu
from jax.sharding import PartitionSpec as P

F32 = jnp.float32
BF16 = jnp.bfloat16
MESH = pl.DeviceIdType.MESH
CORES = 2
QUARTER = 4
FILTER_SEND = 1
FILTER_FORWARD = 2
STEPS = 2
CHUNK_CHANNELS = 4


def split_np(values):
    high = values.astype(np.float32).astype(jnp.bfloat16)
    low = (values - high.astype(np.float64)).astype(np.float32).astype(jnp.bfloat16)
    return high, low


def trig(rows, columns, period):
    product = np.outer(np.arange(rows), np.arange(columns)) % period
    angle = 2.0 * np.pi * product / period
    return np.cos(angle), np.sin(angle)


def tables(seq, lanes):
    n1 = QUARTER * seq
    total = n1 * lanes
    c1, s1 = trig(n1, n1, n1)
    c2, s2 = trig(lanes, lanes, lanes)
    ct, st = trig(n1, lanes, total)
    n1_of = np.arange(n1).reshape(seq, QUARTER)
    zeros = np.zeros((n1, seq, QUARTER))
    top_v = np.concatenate([c1[:, n1_of], zeros], axis=2).reshape(n1, 2 * n1)
    bot_v = np.concatenate([-s1[:, n1_of], zeros], axis=2).reshape(n1, 2 * n1)
    top_d = np.concatenate([zeros, c1[:, n1_of]], axis=2).reshape(n1, 2 * n1)
    bot_d = np.concatenate([zeros, s1[:, n1_of]], axis=2).reshape(n1, 2 * n1)
    forward1 = np.concatenate([top_v, bot_v, top_d, bot_d], axis=0)
    forward_re = np.concatenate([c2, s2], axis=0)
    forward_im = np.concatenate([c2, -s2], axis=0)
    filter2 = np.block([[c2, -s2], [s2, c2]])
    inverse2 = np.block([[c2, s2, c2, -s2], [-s2, c2, s2, c2]])
    zero = np.zeros((n1, n1))
    conv_rows = np.concatenate([c1, -s1, zero, zero], axis=1) / total
    value_rows = np.concatenate([zero, zero, -s1, c1], axis=1) / total
    inverse1 = np.stack(
        [conv_rows.reshape(seq, QUARTER, 4 * n1), value_rows.reshape(seq, QUARTER, 4 * n1)],
        axis=1,
    ).reshape(2 * n1, 4 * n1)
    halves = [
        part
        for matrix in (forward1, forward_re, forward_im, filter2, inverse2, inverse1)
        for part in split_np(matrix)
    ]
    return halves + [ct.astype(np.float32), st.astype(np.float32)]


def split(values):
    high = values.astype(BF16)
    return high, (values - high.astype(F32)).astype(BF16)


def dot3(a, b, dims=((1,), (0,))):
    def one(x, y):
        return lax.dot_general(x, y, (dims, ((), ())), preferred_element_type=F32)

    return one(a[0], b[0]) + one(a[0], b[1]) + one(a[1], b[0])


def build_kernel(dp, seq, channels, lanes, token_total, table_shapes):
    cc = CHUNK_CHANNELS
    width = cc * seq
    chunks = channels // width
    rows = QUARTER * lanes
    n1 = QUARTER * seq
    dp_rows = channels // dp
    half_rows = dp_rows // CORES
    chips = seq // CORES
    rounds = chunks // 2
    groups = chips // 4
    piece = half_rows // groups
    assert rounds * cc == dp and groups * 4 == chips and piece * groups == half_rows
    scale = 1.0 / math.sqrt(token_total)

    def kernel(
        tok_hbm, w_hbm, filt_hbm, cot_hbm,
        f1h_x, f1l_x, frh_x, frl_x, fih_x, fil_x, g2h_x, g2l_x,
        i2h_x, i2l_x, i1h_x, i1l_x, ct_x, st_x,
        mixed_hbm, token_grad_hbm, weight_grad_hbm,
        f1h, f1l, frh, frl, fih, fil, g2h, g2l, i2h, i2l, i1h, i1l, ct, st,
        tok, w_in, filt, cot, mixed, token_grad, weight_grad,
        wall, wh, wl, th, tl, tth, ttl, gate,
        fsend, frecv, bsend, brecv,
        ftmp, ffs, fall, spec,
        wg, sib, rsend, rrecv, rsum, precv, agsend, agrecv,
        in_s, table_s, mixed_s, out_s,
        wy_s, wy_r, wx_s, wx_r, wc_s, wc_r, ff_s, ff_r, fy_s, fy_r, fg_s, fg_r, fs, fr, bs, br,
        sib_s, sib_r, rs_s, rs_r, p_s, p_r, ag_s, ag_r,
    ):
        me_dp = lax.axis_index("dp")
        me = lax.axis_index("seq")
        core = lax.rem(me, CORES)
        chip = me // CORES
        other = CORES - 1 - core
        sibling = chip * CORES + other
        column = me_dp // 2
        row = lax.rem(me_dp, 2)
        partner = column * 2 + 1 - row

        def remote(src, dst, send, recv, d, s):
            return pltpu.make_async_remote_copy(
                src_ref=src, dst_ref=dst, send_sem=send, recv_sem=recv,
                device_id=(d, s), device_id_type=MESH,
            )

        def wait_bytes(ref, sem):
            pltpu.make_async_copy(ref, ref, sem).wait()

        pair_chunk = me_dp // cc
        pair_row = lax.rem(me_dp, cc)
        begin = pl.multiple_of(2 * pair_chunk * width, width)
        inputs = [
            pltpu.make_async_copy(w_hbm, w_in, in_s.at[0]),
            pltpu.make_async_copy(filt_hbm.at[:, pl.ds(begin, 2 * width)], filt, in_s.at[1]),
            pltpu.make_async_copy(tok_hbm.at[0], tok, in_s.at[2]),
            pltpu.make_async_copy(cot_hbm.at[0], cot, in_s.at[3]),
        ]
        sources = [
            f1h_x, f1l_x, frh_x, frl_x, fih_x, fil_x, g2h_x, g2l_x,
            i2h_x, i2l_x, i1h_x, i1l_x, ct_x, st_x,
        ]
        targets = [f1h, f1l, frh, frl, fih, fil, g2h, g2l, i2h, i2l, i1h, i1l, ct, st]
        constants = [
            pltpu.make_async_copy(source, target, table_s.at[k])
            for k, (source, target) in enumerate(zip(sources, targets))
        ]
        for copy in inputs + constants:
            copy.start()

        barrier = pltpu.get_barrier_semaphore()

        @pl.loop(1, seq)
        def _(i):
            pl.semaphore_signal(
                barrier, inc=1, device_id=(me_dp, lax.rem(me + i, seq)), device_id_type=MESH
            )

        @pl.loop(1, dp)
        def _(i):
            pl.semaphore_signal(
                barrier, inc=1, device_id=(lax.rem(me_dp + i, dp), me), device_id_type=MESH
            )

        inputs[0].wait()
        for q in range(chunks):
            for h in range(2):
                begin = h * channels + q * width
                wall[q, me_dp, core, :, h * width : (h + 1) * width] = w_in[
                    pl.ds(pl.multiple_of(core * half_rows, 8), half_rows), begin : begin + width
                ]

        pl.semaphore_wait(barrier, seq - 1 + dp - 1)

        def send_along(block, send, recv):
            @pl.loop(1, dp // 2)
            def _(i):
                target = lax.rem(column + i, dp // 2) * 2 + row
                remote(block, block, send, recv, target, me).start()

        def weights_pair(q):
            block = wall.at[q, me_dp, core]
            remote(block, block, wy_s.at[q], wy_r.at[q], partner, me).start()

        def weights_own(q):
            send_along(wall.at[q, me_dp, core], wx_s.at[q], wx_r.at[q])

        def weights_forward(q):
            block = wall.at[q, partner, core]
            wait_bytes(block, wy_r.at[q])
            send_along(block, wx_s.at[q], wx_r.at[q])

        def weights_share(q):
            wait_bytes(wall.at[q, 0 : dp - 2, 0], wx_r.at[q])
            block = wall.at[q, :, core]
            remote(block, block, wc_s.at[q], wc_r.at[q], me_dp, sibling).start()

        weights_pair(0)
        weights_own(0)

        @pl.loop(1, chunks)
        def _(q):
            weights_pair(q)

        inputs[1].wait()
        for part in range(2):
            for j in range(QUARTER):
                ftmp[j] = filt[
                    j * lanes : (j + 1) * lanes, part * width : (part + 1) * width
                ].T
            for j in range(QUARTER):
                ffs[pl.ds(part * QUARTER + j, seq, stride=2 * QUARTER), :] = ftmp[
                    j, pl.ds(pl.multiple_of(pair_row * seq, seq), seq), :
                ]

        eight = 2 * QUARTER
        weights_forward(0)
        weights_own(1)
        inputs[2].wait()
        high, low = split(tok[...])
        th[...] = high
        tl[...] = low
        inputs[3].wait()
        weights_share(0)
        weights_forward(1)
        pltpu.make_async_copy(
            ffs.at[pl.ds(me * eight, eight), :],
            fall.at[me_dp, pl.ds(me * eight, eight), :],
            ff_r,
        ).start()

        @pl.loop(1, seq)
        def _(i):
            target = lax.rem(me + i, seq)
            remote(
                ffs.at[pl.ds(target * eight, eight), :],
                fall.at[me_dp, pl.ds(me * eight, eight), :],
                ff_s, ff_r, me_dp, target,
            ).start()

        def exchange(source, target_ref, q, send, recv):
            pltpu.make_async_copy(
                source.at[q, :, pl.ds(me * eight, eight), :],
                target_ref.at[q, :, pl.ds(me * eight, eight), :],
                recv.at[q],
            ).start()

            @pl.loop(1, seq)
            def _(i):
                target = lax.rem(me + i, seq)
                remote(
                    source.at[q, :, pl.ds(target * eight, eight), :],
                    target_ref.at[q, :, pl.ds(me * eight, eight), :],
                    send.at[q], recv.at[q], me_dp, target,
                ).start()

        @pl.loop(0, chunks)
        def _(q):
            wait_bytes(wall.at[q, :, other], wc_r.at[q])
            w_high, w_low = split(wall[q].reshape(channels, 2 * width))
            wh[q] = w_high
            wl[q] = w_low
            projected = dot3((th[...], tl[...]), (w_high, w_low))
            gates = projected[:, width:]
            gate[q] = gates
            conv_grad = cot[:, pl.ds(pl.multiple_of(q * width, width), width)] * gates
            for part, values in ((0, projected[:, :width]), (1, conv_grad)):
                for j in range(QUARTER):
                    turned = values[j * lanes : (j + 1) * lanes].T
                    for c in range(cc):
                        fsend[q, c, pl.ds(part * QUARTER + j, seq, stride=eight), :] = turned[
                            c * seq : (c + 1) * seq
                        ]

            @pl.when(q < chunks - 1)
            def _():
                weights_share(q + 1)

            @pl.when(q < chunks - 2)
            def _():
                weights_own(q + 2)
                weights_forward(q + 2)

            @pl.when(q == FILTER_SEND)
            def _():
                wait_bytes(fall.at[me_dp], ff_r)
                block = fall.at[me_dp]
                remote(block, block, fy_s, fy_r, partner, me).start()
                send_along(block, fg_s, fg_r)

            @pl.when(q == FILTER_FORWARD)
            def _():
                wait_bytes(fall.at[partner], fy_r)
                send_along(fall.at[partner], fg_s, fg_r)

            exchange(fsend, frecv, q, fs, fr)

        for j in range(QUARTER):
            for k in range(chunks):
                block = tok[j * lanes : (j + 1) * lanes, k * width : (k + 1) * width].T
                high, low = split(block)
                tth[k * width : (k + 1) * width, j * lanes : (j + 1) * lanes] = high
                ttl[k * width : (k + 1) * width, j * lanes : (j + 1) * lanes] = low

        for copy in constants:
            copy.wait()
        cos_t = ct[...]
        sin_t = st[...]

        def columns(blocks):
            return jnp.concatenate(blocks, axis=1)

        def forward_first(blocks):
            out = dot3((f1h[...], f1l[...]), split(columns(blocks)))
            parts = []
            for c in range(cc):
                lane = out[:, c * lanes : (c + 1) * lanes]
                parts.append([lane[k * n1 : (k + 1) * n1] for k in range(4)])
            return parts

        wait_bytes(fall.at[0 : dp - 2], fg_r)

        @pl.loop(0, chunks // 2)
        def _(p):
            parts = forward_first([fall[p * cc + c] for c in range(cc)])
            for part in range(2):
                stacked = []
                for c in range(cc):
                    real, imag = parts[c][2 * part], parts[c][2 * part + 1]
                    if part == 1:
                        imag = -imag
                    stacked.append(
                        columns([real * cos_t + imag * sin_t, imag * cos_t - real * sin_t])
                    )
                spec[2 * p + part] = dot3(
                    split(jnp.concatenate(stacked, axis=0)), (g2h[...], g2l[...])
                )

        @pl.loop(0, chunks)
        def _(q):
            wait_bytes(frecv.at[q], fr.at[q])
            parts = forward_first([frecv[q, c] for c in range(cc)])
            re_in, im_in = [], []
            for c in range(cc):
                a, b, e, f = parts[c]
                a, b = a * cos_t + b * sin_t, b * cos_t - a * sin_t
                e, f = e * cos_t - f * sin_t, f * cos_t + e * sin_t
                re_in.append(columns([a - f, b - e]))
                im_in.append(columns([b + e, a + f]))
            real = dot3(split(jnp.concatenate(re_in, axis=0)), (frh[...], frl[...]))
            imag = dot3(split(jnp.concatenate(im_in, axis=0)), (fih[...], fil[...]))
            h_real = spec[q, :, :lanes]
            h_imag = spec[q, :, lanes:]
            product = columns([real * h_real - imag * h_imag, real * h_imag + imag * h_real])
            inner = dot3(split(product), (i2h[...], i2l[...]))
            out_in = []
            for c in range(cc):
                block = inner[c * n1 : (c + 1) * n1]
                g, h, g2, h2 = [block[:, k * lanes : (k + 1) * lanes] for k in range(4)]
                out_in.append(
                    jnp.concatenate(
                        [
                            g * cos_t - h * sin_t,
                            h * cos_t + g * sin_t,
                            g2 * cos_t + h2 * sin_t,
                            h2 * cos_t - g2 * sin_t,
                        ],
                        axis=0,
                    )
                )
            result = dot3((i1h[...], i1l[...]), split(columns(out_in)))
            for c in range(cc):
                bsend[q, c] = result[:, c * lanes : (c + 1) * lanes]

            @pl.when(q < 2)
            def _():
                exchange(bsend, brecv, q, bs, br)

        def reduce_dp(q):
            wait_bytes(sib.at[q], sib_r.at[q])
            total = wg[q, :, core] + sib[q]
            rsend[q] = total
            pltpu.make_async_copy(rsend.at[q, me_dp], rrecv.at[q, me_dp], rs_r.at[q]).start()

            @pl.loop(1, dp)
            def _(i):
                target = lax.rem(me_dp + i, dp)
                remote(
                    rsend.at[q, target], rrecv.at[q, me_dp],
                    rs_s.at[q], rs_r.at[q], target, me,
                ).start()

        def sum_dp(q):
            wait_bytes(rrecv.at[q], rs_r.at[q])
            total = rrecv[q, 0]
            for k in range(1, dp):
                total = total + rrecv[q, k]
            for g in range(groups):
                for h in range(2):
                    rsum[q // 2, lax.rem(q, 2) * 2 * groups + 2 * g + h] = total[
                        g * piece : (g + 1) * piece, h * width : (h + 1) * width
                    ]

        def scatter_seq(r):
            pltpu.make_async_copy(rsum.at[r, chip], precv.at[r, chip], p_r.at[r]).start()

            @pl.loop(1, chips)
            def _(i):
                target = lax.rem(chip + i, chips)
                remote(
                    rsum.at[r, target], precv.at[r, chip],
                    p_s.at[r], p_r.at[r], me_dp, target * CORES + core,
                ).start()

        def gather_seq(r):
            wait_bytes(precv.at[r], p_r.at[r])
            total = precv[r, 0]
            for k in range(1, chips):
                total = total + precv[r, k]
            agsend[r] = total * scale
            pltpu.make_async_copy(agsend.at[r], agrecv.at[r, me], ag_r.at[r]).start()

            @pl.loop(1, seq)
            def _(i):
                remote(
                    agsend.at[r], agrecv.at[r, me],
                    ag_s.at[r], ag_r.at[r], me_dp, lax.rem(me + i, seq),
                ).start()

        @pl.loop(0, chunks)
        def _(q):
            wait_bytes(brecv.at[q], br.at[q])
            results = []
            for part in range(2):
                blocks = []
                for j in range(QUARTER):
                    turned = jnp.concatenate(
                        [
                            brecv[q, c, pl.ds(part * QUARTER + j, seq, stride=eight), :]
                            for c in range(cc)
                        ],
                        axis=0,
                    )
                    blocks.append(turned.T)
                results.append(jnp.concatenate(blocks, axis=0))
            convolved, d_value = results
            lane = pl.ds(pl.multiple_of(q * width, width), width)
            d_pre = split(columns([d_value, cot[:, lane] * convolved]))
            grad = dot3((tth[...], ttl[...]), d_pre)
            wg[q] = grad.reshape(dp, CORES, half_rows, 2 * width)
            remote(
                wg.at[q, :, CORES - 1 - core], sib.at[q],
                sib_s.at[q], sib_r.at[q], me_dp, sibling,
            ).start()

            @pl.when(q > 0)
            def _():
                reduce_dp(q - 1)

            @pl.when(q < chunks - 2)
            def _():
                exchange(bsend, brecv, q + 2, bs, br)

            mixed[q] = gate[q] * convolved
            pltpu.make_async_copy(mixed.at[q], mixed_hbm.at[0, :, lane], mixed_s.at[q]).start()
            back = dot3(d_pre, (wh[q], wl[q]), ((1,), (1,)))

            @pl.when(q == 0)
            def _():
                token_grad[...] = back

            @pl.when(q > 0)
            def _():
                token_grad[...] = token_grad[...] + back

        grad_copy = pltpu.make_async_copy(token_grad, token_grad_hbm.at[0], out_s.at[0])
        grad_copy.start()
        reduce_dp(chunks - 1)
        for r in range(rounds):
            sum_dp(2 * r)
            sum_dp(2 * r + 1)
            scatter_seq(r)
        for r in range(rounds):
            gather_seq(r)
        for r in range(rounds):
            wait_bytes(agrecv.at[r], ag_r.at[r])
            for s in range(seq):
                p = s // CORES
                q, g, h = 2 * r + p // (2 * groups), (p % (2 * groups)) // 2, p % 2
                row = (s % CORES) * half_rows + g * piece
                column = h * channels + q * width
                weight_grad[row : row + piece, column : column + width] = agrecv[r, s]
        weight_copy = pltpu.make_async_copy(weight_grad, weight_grad_hbm, out_s.at[1])
        weight_copy.start()

        @pl.loop(0, chunks)
        def _(q):
            wait_bytes(wall.at[q, 0, 0], wy_s.at[q])
            wait_bytes(wall.at[q, 0 : dp - 2, 0], wx_s.at[q])
            wait_bytes(wall.at[q, :, 0], wc_s.at[q])
            wait_bytes(fsend.at[q, :, 0 : (seq - 1) * eight, :], fs.at[q])
            wait_bytes(bsend.at[q, :, 0 : (seq - 1) * eight, :], bs.at[q])
            wait_bytes(sib.at[q], sib_s.at[q])
            wait_bytes(rsend.at[q, 0 : dp - 1], rs_s.at[q])

        wait_bytes(ffs.at[0 : (seq - 1) * eight, :], ff_s)
        wait_bytes(fall.at[0], fy_s)
        wait_bytes(fall.at[0 : dp - 2], fg_s)
        for r in range(rounds):
            wait_bytes(rsum.at[r, 0 : chips - 1], p_s.at[r])
            wait_bytes(agrecv.at[r, 0 : seq - 1], ag_s.at[r])

        @pl.loop(0, chunks)
        def _(q):
            lane = pl.ds(pl.multiple_of(q * width, width), width)
            pltpu.make_async_copy(mixed.at[q], mixed_hbm.at[0, :, lane], mixed_s.at[q]).wait()

        grad_copy.wait()
        weight_copy.wait()

    dma = pltpu.SemaphoreType.DMA
    f32, bf16 = F32, BF16
    scratch = [pltpu.VMEM(shape, kind) for shape, kind in table_shapes] + [
        pltpu.VMEM((rows, channels), f32),
        pltpu.VMEM((dp_rows, 2 * channels), f32),
        pltpu.VMEM((rows, 2 * width), f32),
        pltpu.VMEM((rows, channels), f32),
        pltpu.VMEM((chunks, rows, width), f32),
        pltpu.VMEM((rows, channels), f32),
        pltpu.VMEM((dp_rows, 2 * channels), f32),
        pltpu.VMEM((chunks, dp, CORES, half_rows, 2 * width), f32),
        pltpu.VMEM((chunks, channels, 2 * width), bf16),
        pltpu.VMEM((chunks, channels, 2 * width), bf16),
        pltpu.VMEM((rows, channels), bf16),
        pltpu.VMEM((rows, channels), bf16),
        pltpu.VMEM((channels, rows), bf16),
        pltpu.VMEM((channels, rows), bf16),
        pltpu.VMEM((chunks, rows, width), f32),
        pltpu.VMEM((chunks, cc, 2 * n1, lanes), f32),
        pltpu.VMEM((chunks, cc, 2 * n1, lanes), f32),
        pltpu.VMEM((chunks, cc, 2 * n1, lanes), f32),
        pltpu.VMEM((chunks, cc, 2 * n1, lanes), f32),
        pltpu.VMEM((QUARTER, width, lanes), f32),
        pltpu.VMEM((2 * n1, lanes), f32),
        pltpu.VMEM((dp, 2 * n1, lanes), f32),
        pltpu.VMEM((chunks, cc * n1, 2 * lanes), f32),
        pltpu.VMEM((chunks, dp, CORES, half_rows, 2 * width), f32),
        pltpu.VMEM((chunks, dp, half_rows, 2 * width), f32),
        pltpu.VMEM((chunks, dp, half_rows, 2 * width), f32),
        pltpu.VMEM((chunks, dp, half_rows, 2 * width), f32),
        pltpu.VMEM((rounds, chips, piece, width), f32),
        pltpu.VMEM((rounds, chips, piece, width), f32),
        pltpu.VMEM((rounds, piece, width), f32),
        pltpu.VMEM((rounds, seq, piece, width), f32),
        dma((4,)), dma((len(table_shapes),)), dma((chunks,)), dma((2,)),
        dma((chunks,)), dma((chunks,)), dma((chunks,)), dma((chunks,)),
        dma((chunks,)), dma((chunks,)), dma, dma, dma, dma, dma, dma,
        dma((chunks,)), dma((chunks,)), dma((chunks,)), dma((chunks,)),
        dma((chunks,)), dma((chunks,)), dma((chunks,)), dma((chunks,)),
        dma((rounds,)), dma((rounds,)), dma((rounds,)), dma((rounds,)),
    ]
    return kernel, scratch


def shards(dp, seq, tokens, in_weight, filters, cotangent):
    _, rows, channels = tokens.shape
    lanes = rows // QUARTER
    constants = tables(seq, lanes)
    kernel, scratch = build_kernel(
        dp, seq, channels, lanes, dp * seq * rows, [(c.shape, c.dtype) for c in constants]
    )
    whole = pl.BlockSpec(memory_space=pl.ANY)
    shapes = (
        jax.ShapeDtypeStruct(tokens.shape, F32),
        jax.ShapeDtypeStruct(tokens.shape, F32),
        jax.ShapeDtypeStruct(in_weight.shape, F32),
    )

    def place(a, b, c, x, y, z):
        x[...] = a[...]
        y[...] = b[...]
        z[...] = c[...]

    results = pl.pallas_call(
        kernel,
        out_shape=shapes,
        in_specs=[whole] * (4 + len(constants)),
        out_specs=(whole,) * 3,
        scratch_shapes=scratch,
        compiler_params=pltpu.CompilerParams(
            collective_id=0, has_side_effects=True, vmem_limit_bytes=60 * 1024 * 1024
        ),
        name="gated_conv_layer",
    )(tokens, in_weight, filters, cotangent, *[jnp.asarray(c) for c in constants])
    steps = STEPS
    blocks = (
        pl.BlockSpec((1, rows // steps, channels), lambda i: (0, i, 0)),
        pl.BlockSpec((1, rows // steps, channels), lambda i: (0, i, 0)),
        pl.BlockSpec((in_weight.shape[0] // steps, 2 * channels), lambda i: (i, 0)),
    )
    return pl.pallas_call(
        place,
        grid=(steps,),
        out_shape=shapes,
        in_specs=list(blocks),
        out_specs=blocks,
        name="place_results",
    )(*results)


def solution(mesh):
    dp, seq = mesh.shape["dp"], mesh.shape["seq"]

    def local(tokens, in_weight, filters, cotangent):
        return shards(dp, seq, tokens, in_weight, filters, cotangent)

    placed = (P("dp", "seq", None), P("dp", None), P("seq", None), P("dp", "seq", None))
    return jax.shard_map(
        local,
        mesh=mesh,
        in_specs=placed,
        out_specs=(P("dp", "seq", None), P("dp", "seq", None), P("dp", None)),
        check_vma=False,
    )
```
